256 devices in a mesh: grid: 16 (over z_hi, x, core), orb: 16 (over z_lo, y).
Axes of the slice: x: 4, y: 4, z: 8 (z_hi: 2, z_lo: 4; z = z_hi * 4 + z_lo), core: 2. Of those that a mesh axis runs over, the one named last changes fastest.
Arguments:
- psi_window: bfloat16 [3072, 16384], P('orb', 'grid'), may hold values from -6 to 6
- phi_window: bfloat16 [3072, 16384], P('orb', 'grid'), may hold values from -6 to 6
- psi_region: bfloat16 [3072, 98304], P('orb', 'grid'), may hold values from -6 to 6
- phi_region: bfloat16 [3072, 98304], P('orb', 'grid'), may hold values from -6 to 6
- points: int32 [12288], P('grid'), may hold values from 0 to 6143, as said below
Outputs:
- fit_rhs: bfloat16 [16384, 16, 768], P('grid', None, 'orb')
The draws below stay inside these ranges and needn't reach their ends.
Inputs may be any that keep to these rules, and one draw needn't show every extreme that they name: `points`: within each owner's block of 768 entries the indices are distinct; every block holds both 0 and 6143.
All inputs are finite; a program needn't handle non-finite values.
Results may differ from the reference program's by a relative error of at most 0.001.
Values may be sent and summed in bfloat16 or wider, within the bound.
No kernel may reach another device: no remote copies, remote signals or barrier semaphores. Data moves between devices by JAX's collectives and lax.ppermute only.
A program may use at most 128 MiB of HBM per device.

```python
import jax
import jax.numpy as jnp
from jax import lax

NORB = 3072
M_DEV = 768
REG_DEV = 6144
NR = 16384
NREG = 98304
N_GRID = 16


def draw_points(key, part):
    key = jax.random.fold_in(key, 11)

    def one_owner(owner):
        owner_key = jax.random.fold_in(key, owner)
        first_key, second_key = jax.random.split(owner_key)
        inner = jax.random.permutation(first_key, REG_DEV - 2)[:M_DEV - 2].astype(jnp.int32) + 1
        ends = jnp.array([0, REG_DEV - 1], dtype=jnp.int32)
        chosen = jnp.concatenate([ends, inner])
        return jax.random.permutation(second_key, chosen)
    return jax.vmap(one_owner)(jnp.arange(N_GRID, dtype=jnp.int32)).reshape(N_GRID * M_DEV)


def block_levels(rng, extent, shards, least, top_value):
    loudness = 1.0
    for position, shards_of in shards:
        steps = jax.random.uniform(jax.random.fold_in(jax.random.fold_in(rng, 6), position), (shards_of,), jnp.float32, least / len(shards), top_value / len(shards))
        loudness = loudness * jnp.repeat(jnp.exp(steps), extent[position] // shards_of).reshape((-1,) + (1,) * (len(extent) - 1 - position))
    return loudness


def gaussian(rng, shape, deviation, limit, cuts=(), held_as=jnp.bfloat16):
    gain = block_levels(rng, shape, cuts, -0.22, 0.18) if cuts else 1.0
    entries = jax.random.normal(rng, shape, jnp.float32) * deviation * gain
    return jnp.minimum(jnp.maximum(entries, -limit), limit).astype(held_as)


def setup_inputs(seed: int = 0) -> dict:
    key_list = jax.random.split(jax.random.key(seed), 6)
    return {
        "psi_window": gaussian(key_list[0], (NORB, NR), 1.0, 6.0, ((0, 16), (1, 16))),
        "phi_window": gaussian(key_list[1], (NORB, NR), 1.0, 6.0, ((0, 16), (1, 16))),
        "psi_region": gaussian(key_list[2], (NORB, NREG), 1.0, 6.0, ((0, 16), (1, 16))),
        "phi_region": gaussian(key_list[3], (NORB, NREG), 1.0, 6.0, ((0, 16), (1, 16))),
        "points": draw_points(jax.random.fold_in(key_list[5], 71), 0),
    }


def reference(psi_window, phi_window, psi_region, phi_region, points):
    offsets = (jnp.arange(N_GRID, dtype=jnp.int32) * REG_DEV)[:, None]
    columns = points.reshape(N_GRID, M_DEV).astype(jnp.int32) + offsets

    def one_owner(index_row):
        psi_at = jnp.take(psi_region, index_row, axis=1)
        phi_at = jnp.take(phi_region, index_row, axis=1)
        occ_gram = jnp.dot(psi_window.T, psi_at, preferred_element_type=jnp.float32)
        emp_gram = jnp.dot(phi_window.T, phi_at, preferred_element_type=jnp.float32)
        return (occ_gram * emp_gram / NORB).astype(jnp.bfloat16)

    stacked = lax.map(one_owner, columns)
    return jnp.transpose(stacked, (1, 0, 2))
```

```python
import functools

import jax
import jax.numpy as jnp
from jax import lax
from jax.experimental import pallas as pl
from jax.experimental.pallas import tpu as pltpu
from jax.sharding import Mesh, PartitionSpec as P

AXES = ("zhi", "x", "core", "zlo", "y")
SIZES = {"zhi": 2, "x": 4, "core": 2, "zlo": 4, "y": 4}
GRID = ("zhi", "x", "core")
ORB = ("zlo", "y")

NPTS = 768
SHARE = 48
ORBS = 192
REGION = 6144
ROWS = 1024
KSLOT = 4 * ORBS
CHUNK = 1024
VMEM_LIMIT = 56 * 1024 * 1024


def shift(value, axis, step):
    n = SIZES[axis]
    return lax.ppermute(value, axis, [(i, (i + step) % n) for i in range(n)])


def gather_kernel(points_ref, psi_ref, phi_ref, out_ref, acc_ref):
    step = pl.program_id(0)
    columns = lax.broadcasted_iota(jnp.int32, (NPTS, CHUNK), 1) + step * CHUNK
    pick = jnp.where(points_ref[...] == columns, 1.0, 0.0).astype(jnp.bfloat16)
    both = jnp.concatenate([psi_ref[...], phi_ref[...]], axis=0)
    part = lax.dot_general(
        pick, both, (((1,), (1,)), ((), ())), preferred_element_type=jnp.float32
    )

    @pl.when(step == 0)
    def _():
        acc_ref[...] = part

    @pl.when(step > 0)
    def _():
        acc_ref[...] += part

    @pl.when(step == pl.num_programs(0) - 1)
    def _():
        out_ref[...] = acc_ref[...].astype(jnp.bfloat16)


def gather_points(points, psi_region, phi_region):
    steps = REGION // CHUNK
    return pl.pallas_call(
        gather_kernel,
        grid=(steps,),
        in_specs=[
            pl.BlockSpec((NPTS, 1), lambda j: (0, 0)),
            pl.BlockSpec((ORBS, CHUNK), lambda j: (0, j)),
            pl.BlockSpec((ORBS, CHUNK), lambda j: (0, j)),
        ],
        out_specs=pl.BlockSpec((NPTS, 2 * ORBS), lambda j: (0, 0)),
        out_shape=jax.ShapeDtypeStruct((NPTS, 2 * ORBS), jnp.bfloat16),
        scratch_shapes=[pltpu.VMEM((NPTS, 2 * ORBS), jnp.float32)],
        compiler_params=pltpu.CompilerParams(vmem_limit_bytes=VMEM_LIMIT),
        cost_estimate=pl.CostEstimate(
            flops=2 * NPTS * REGION * 2 * ORBS, bytes_accessed=2 * ORBS * REGION * 2, transcendentals=0
        ),
        name="gather_points",
    )(points, psi_region, phi_region)


def gram_kernel(slots, first, last, pos_ref, *refs):
    n_w = 5 * len(slots)
    w_refs, refs = refs[:n_w], refs[n_w:]
    p_refs, refs = refs[:10], refs[10:]
    if not first:
        acc_in, refs = refs[0], refs[1:]
    out_ref, w_buf, p_buf, acc, w_sem, p_sem, a_sem = refs
    x, core, zlo, y = pos_ref[0], pos_ref[1], pos_ref[2], pos_ref[3]

    copies = []
    for s, slot in enumerate(slots):
        mine = []
        own, ym, yp, fm, fp = w_refs[5 * s : 5 * s + 5]
        for j, (ref, e) in enumerate(((own, 0), (ym, 3), (yp, 1))):
            mine.append(pltpu.make_async_copy(ref, w_buf.at[s, :, (y + e) % 4], w_sem.at[s, j]))
        for j, ref in enumerate((fm, fp)):
            mine.append(pltpu.make_async_copy(ref, w_buf.at[s, j, (y + 2) % 4], w_sem.at[s, 3 + j]))
        zsel = (zlo - slot + 4) % 4
        for swap in range(2):
            who = (core + swap) % 2
            own, dm, dp, f1, f2 = p_refs[5 * swap : 5 * swap + 5]
            for zhi in range(2):
                for j, (ref, e) in enumerate(((own, 0), (dm, 3), (dp, 1))):
                    mine.append(
                        pltpu.make_async_copy(
                            ref.at[zhi * 4 + zsel],
                            p_buf.at[s, zhi * 8 + ((x + e) % 4) * 2 + who],
                            p_sem.at[s, swap, zhi, j],
                        )
                    )
                mine.append(
                    pltpu.make_async_copy(
                        (f1, f2)[zhi].at[zsel],
                        p_buf.at[s, zhi * 8 + ((x + 2) % 4) * 2 + who],
                        p_sem.at[s, swap, zhi, 3],
                    )
                )
        for copy in mine:
            copy.start()
        copies.append(mine)
    if not first:
        load = pltpu.make_async_copy(acc_in, acc, a_sem)
        load.start()

    tile = 256
    for s in range(len(slots)):
        for copy in copies[s]:
            copy.wait()
        if s == 0 and not first:
            load.wait()

        def body(n, _):
            cols = pl.ds(pl.multiple_of(n * tile, tile), tile)
            grams = []
            for m in range(2):
                lhs = p_buf[s, :, :, m * KSLOT : (m + 1) * KSLOT].reshape(NPTS, KSLOT)
                rhs = w_buf[s, m, :, :, cols].reshape(KSLOT, tile)
                part = jnp.dot(lhs, rhs, preferred_element_type=jnp.float32)
                if not (first and s == 0):
                    part += acc[m, :, cols]
                grams.append(part)
            if last and s == len(slots) - 1:
                fitted = grams[0] * grams[1] * (1.0 / (16 * ORBS))
                out_ref[:, cols] = fitted.astype(jnp.bfloat16)
            else:
                for m in range(2):
                    acc[m, :, cols] = grams[m]
            return 0

        lax.fori_loop(0, ROWS // tile, body, 0)
    if not last:
        store = pltpu.make_async_copy(acc, out_ref, a_sem)
        store.start()
        store.wait()


def gram(slots, first, last, pos, w_parts, p_parts, acc=None):
    n = len(slots)
    any_spec = pl.BlockSpec(memory_space=pl.ANY)
    operands = list(w_parts) + list(p_parts) + ([] if first else [acc])
    if last:
        out_shape = jax.ShapeDtypeStruct((NPTS, ROWS), jnp.bfloat16)
        out_spec = pl.BlockSpec(memory_space=pltpu.VMEM)
    else:
        out_shape = jax.ShapeDtypeStruct((2, NPTS, ROWS), jnp.float32)
        out_spec = any_spec
    return pl.pallas_call(
        functools.partial(gram_kernel, slots, first, last),
        in_specs=[pl.BlockSpec(memory_space=pltpu.SMEM)] + [any_spec] * len(operands),
        out_specs=out_spec,
        out_shape=out_shape,
        scratch_shapes=[
            pltpu.VMEM((n, 2, 4, ORBS, ROWS), jnp.bfloat16),
            pltpu.VMEM((n, 16, SHARE, 2 * KSLOT), jnp.bfloat16),
            pltpu.VMEM((2, NPTS, ROWS), jnp.float32),
            pltpu.SemaphoreType.DMA((n, 5)),
            pltpu.SemaphoreType.DMA((n, 2, 2, 4)),
            pltpu.SemaphoreType.DMA,
        ],
        compiler_params=pltpu.CompilerParams(vmem_limit_bytes=VMEM_LIMIT),
        cost_estimate=pl.CostEstimate(
            flops=2 * 2 * n * NPTS * KSLOT * ROWS, bytes_accessed=n * 6 * 2**20, transcendentals=0
        ),
        name="gram_last" if last else "gram_first",
    )(pos, *operands)


def per_device(psi_window, phi_window, psi_region, phi_region, points):
    pos = jnp.stack([lax.axis_index(a) for a in ("x", "core", "zlo", "y")]).astype(jnp.int32)

    own = jnp.stack([psi_window, phi_window])
    slots = [own] + [shift(own, "zlo", d) for d in (1, 2, 3)]
    w_parts = []
    for slot in slots:
        below, above = shift(slot, "y", 1), shift(slot, "y", -1)
        far_psi, far_phi = shift(below[0], "y", 1), shift(above[1], "y", -1)
        w_parts.append((slot, below, above, far_psi, far_phi))

    order = points.reshape(4, 4, SHARE).transpose(1, 0, 2).reshape(NPTS, 1)
    picked = gather_points(order, psi_region, phi_region).reshape(4, 4, SHARE, 2 * ORBS)
    by_y = lax.all_to_all(picked, "y", 0, 0, tiled=True)
    cols = by_y.reshape(4, 4, SHARE, 2, ORBS).transpose(1, 2, 3, 0, 4).reshape(4, SHARE, 2 * KSLOT)
    both = jnp.concatenate([cols, cols])
    mine = lax.all_to_all(both, ("zhi", "zlo"), 0, 0, tiled=True)
    below, above = shift(mine, "x", 1), shift(mine, "x", -1)
    far_lo, far_hi = shift(below[:4], "x", 1), shift(above[4:], "x", -1)
    p_parts = [mine, below, above, far_lo, far_hi]
    p_parts += [shift(part, "core", 1) for part in p_parts]

    acc = gram((0, 1, 2), True, False, pos, w_parts[0] + w_parts[1] + w_parts[2], p_parts)
    out = gram((3,), False, True, pos, w_parts[3], p_parts, acc)
    return out.reshape(16, SHARE, ROWS).transpose(2, 0, 1)


def solution(mesh):
    torus = Mesh(mesh.devices.reshape(tuple(SIZES[a] for a in AXES)), AXES)
    in_specs = (P(ORB, GRID), P(ORB, GRID), P(ORB, GRID), P(ORB, GRID), P(GRID))
    out_specs = P(GRID, None, ORB)
    return jax.shard_map(
        per_device, mesh=torus, in_specs=in_specs, out_specs=out_specs, check_vma=False
    )
```

```python
import functools

import jax
import jax.numpy as jnp
from jax import lax
from jax.experimental import pallas as pl
from jax.experimental.pallas import tpu as pltpu
from jax.sharding import Mesh, PartitionSpec as P

AXES = ("zhi", "x", "core", "zlo", "y")
SIZES = {"zhi": 2, "x": 4, "core": 2, "zlo": 4, "y": 4}
GRID = ("zhi", "x", "core")
ORB = ("zlo", "y")

NPTS = 768
SHARE = 48
ORBS = 192
HALF = ORBS // 2
REGION = 6144
ROWS = 1024
KSLOT = 4 * ORBS
CHUNK = 1024
TILE = 512
GROUPS = ((0,), (1, 2, 3))
MIB = 1024 * 1024

PAIRS = [(0, 1), (1, 0), (2, 3), (3, 2)]
MIRROR = [(0, 3), (1, 2), (2, 1), (3, 0)]


def shift(value, axis, step):
    n = SIZES[axis]
    return lax.ppermute(value, axis, [(i, (i + step) % n) for i in range(n)])


def after(value, *others):
    return lax.optimization_barrier((value,) + others)[0]


def gather_kernel(points_ref, psi_ref, phi_ref, out_ref, acc_ref):
    step = pl.program_id(0)
    columns = lax.broadcasted_iota(jnp.int32, (NPTS, CHUNK), 1) + step * CHUNK
    pick = jnp.where(points_ref[...] == columns, 1.0, 0.0).astype(jnp.bfloat16)
    both = jnp.concatenate([psi_ref[...], phi_ref[...]], axis=0)
    part = lax.dot_general(
        pick, both, (((1,), (1,)), ((), ())), preferred_element_type=jnp.float32
    )

    @pl.when(step == 0)
    def _():
        acc_ref[...] = part

    @pl.when(step > 0)
    def _():
        acc_ref[...] += part

    @pl.when(step == pl.num_programs(0) - 1)
    def _():
        out_ref[...] = acc_ref[...].astype(jnp.bfloat16)


def gather_points(points, psi_region, phi_region):
    steps = REGION // CHUNK
    return pl.pallas_call(
        gather_kernel,
        grid=(steps,),
        in_specs=[
            pl.BlockSpec((NPTS, 1), lambda j: (0, 0)),
            pl.BlockSpec((ORBS, CHUNK), lambda j: (0, j)),
            pl.BlockSpec((ORBS, CHUNK), lambda j: (0, j)),
        ],
        out_specs=pl.BlockSpec((NPTS, 2 * ORBS), lambda j: (0, 0)),
        out_shape=jax.ShapeDtypeStruct((NPTS, 2 * ORBS), jnp.bfloat16),
        scratch_shapes=[pltpu.VMEM((NPTS, 2 * ORBS), jnp.float32)],
        compiler_params=pltpu.CompilerParams(vmem_limit_bytes=56 * MIB),
        cost_estimate=pl.CostEstimate(
            flops=2 * NPTS * REGION * 2 * ORBS, bytes_accessed=2 * ORBS * REGION * 2, transcendentals=0
        ),
        name="gather_points",
    )(points, psi_region, phi_region)


def spread_kernel(in_ref, out_ref):
    for y in range(4):
        for m in range(2):
            out_ref[m, :, :, y * ORBS : (y + 1) * ORBS] = in_ref[y, :, :, m * ORBS : (m + 1) * ORBS]


def join_orbitals(by_y):
    return pl.pallas_call(
        spread_kernel,
        in_specs=[pl.BlockSpec(memory_space=pltpu.VMEM)],
        out_specs=pl.BlockSpec(memory_space=pltpu.VMEM),
        out_shape=jax.ShapeDtypeStruct((2, 4, SHARE, KSLOT), jnp.bfloat16),
        compiler_params=pltpu.CompilerParams(vmem_limit_bytes=8 * MIB),
        name="join_orbitals",
    )(by_y)


def gram_kernel(pieces, n_w, pos_ref, *refs):
    w_refs, p_refs = refs[:n_w], refs[n_w : n_w + 10]
    out_ref, w_buf, p_buf, acc, w_sem, p_sem = refs[n_w + 10 :]
    x, core, zlo, y = pos_ref[0], pos_ref[1], pos_ref[2], pos_ref[3]
    pair = zlo + 1 - 2 * (zlo % 2)
    which = [zlo, pair, 3 - zlo, 3 - pair]

    def loads(s):
        mine = []
        for j, (ref, source, m, e, rows) in enumerate(pieces[s]):
            mine.append(
                pltpu.make_async_copy(
                    w_refs[ref].at[source], w_buf.at[s, m, (y + e) % 4, rows], w_sem.at[s, j]
                )
            )
        for swap in range(2):
            who = (core + swap) % 2
            five = p_refs[5 * swap : 5 * swap + 5]
            for j, e in enumerate((0, 3, 1)):
                mine.append(
                    pltpu.make_async_copy(
                        five[j].at[:, which[s]], p_buf.at[s, :, (x + e) % 4, who], p_sem.at[s, swap, j]
                    )
                )
            for m in range(2):
                mine.append(
                    pltpu.make_async_copy(
                        five[3 + m].at[:, which[s]],
                        p_buf.at[s, :, (x + 2) % 4, who, m],
                        p_sem.at[s, swap, 3 + m],
                    )
                )
        return mine

    copies = [loads(s) for s in range(4)]
    for copy in copies[0]:
        copy.start()
    for i, group in enumerate(GROUPS):
        for s in group:
            for copy in copies[s]:
                copy.wait()
            if s == 0:
                for later in copies[1:]:
                    for copy in later:
                        copy.start()
        last = i == len(GROUPS) - 1

        def body(n, _):
            cols = pl.ds(pl.multiple_of(n * TILE, TILE), TILE)
            grams = []
            for m in range(2):
                lhs = jnp.concatenate([p_buf[s, :, :, :, m].reshape(NPTS, KSLOT) for s in group], axis=1)
                rhs = w_buf[group[0] : group[-1] + 1, m, :, :, cols].reshape(len(group) * KSLOT, TILE)
                part = jnp.dot(lhs, rhs, preferred_element_type=jnp.float32)
                grams.append(part if i == 0 else part + acc[m, :, cols])
            if last:
                fitted = grams[0] * grams[1] * (1.0 / (16 * ORBS))
                out_ref[:, cols] = fitted.astype(jnp.bfloat16)
            else:
                for m in range(2):
                    acc[m, :, cols] = grams[m]
            return 0

        lax.fori_loop(0, ROWS // TILE, body, 0)


def gram(pos, parts, p_parts):
    arrays, pieces = [], []
    for slot in parts:
        mine = []
        for array, *place in slot:
            found = [i for i, a in enumerate(arrays) if a is array]
            if not found:
                found = [len(arrays)]
                arrays.append(array)
            mine.append((found[0], *place))
        pieces.append(mine)
    any_spec = pl.BlockSpec(memory_space=pl.ANY)
    p_parts = [p.reshape((2, 4) + p.shape[1:]) for p in p_parts]
    return pl.pallas_call(
        functools.partial(gram_kernel, pieces, len(arrays)),
        in_specs=[pl.BlockSpec(memory_space=pltpu.SMEM)] + [any_spec] * (len(arrays) + 10),
        out_specs=pl.BlockSpec(memory_space=pltpu.VMEM),
        out_shape=jax.ShapeDtypeStruct((NPTS, ROWS), jnp.bfloat16),
        scratch_shapes=[
            pltpu.VMEM((4, 2, 4, ORBS, ROWS), jnp.bfloat16),
            pltpu.VMEM((4, 2, 4, 2, 2, SHARE, KSLOT), jnp.bfloat16),
            pltpu.VMEM((2, NPTS, ROWS), jnp.float32),
            pltpu.SemaphoreType.DMA((4, max(len(slot) for slot in pieces))),
            pltpu.SemaphoreType.DMA((4, 2, 5)),
        ],
        compiler_params=pltpu.CompilerParams(vmem_limit_bytes=48 * MIB),
        cost_estimate=pl.CostEstimate(
            flops=2 * 2 * 4 * NPTS * KSLOT * ROWS, bytes_accessed=24 * MIB, transcendentals=0
        ),
        name="gram",
    )(pos, *arrays, *p_parts)


def per_device(psi_window, phi_window, psi_region, phi_region, points):
    pos = jnp.stack([lax.axis_index(a) for a in ("x", "core", "zlo", "y")]).astype(jnp.int32)
    both, full, one, two = slice(0, 2), slice(0, ORBS), slice(1, 3), slice(0, 2)
    parts = [[] for _ in range(4)]

    own = jnp.stack([psi_window, phi_window])
    below, above = shift(own, "y", 1), shift(own, "y", -1)
    near = lax.ppermute(own, "zlo", PAIRS)
    mirror = lax.ppermute(own, "zlo", MIRROR)
    parts[0] += [(own, both, both, 0, full), (below, both, both, 3, full), (above, both, both, 1, full)]

    def ring(s, slot, below, above):
        up = shift(jnp.concatenate([below[0:1], slot]), "y", 1)
        down = shift(jnp.concatenate([slot, above[1:2]]), "y", -1)
        parts[s - 1] += [(up, 0, 0, 2, full), (down, 2, 1, 2, full)]
        parts[s] += [(slot, both, both, 0, full), (up, one, both, 3, full), (down, two, both, 1, full)]
        return up[1:], down[:2]

    order = points.reshape(4, 4, SHARE).transpose(1, 0, 2).reshape(NPTS, 1)
    picked = gather_points(order, psi_region, phi_region).reshape(4, 4, SHARE, 2 * ORBS)
    cols = join_orbitals(lax.all_to_all(picked, "y", 0, 0, tiled=True))
    cols = after(cols, below, above, near, mirror)

    below, above = ring(1, near, below, above)
    cols = cols.transpose(1, 0, 2, 3)
    mine = lax.all_to_all(jnp.concatenate([cols, cols]), ("zhi", "zlo"), 0, 0, tiled=True)
    mine = after(mine, below, above, mirror)

    below, above = ring(2, mirror, below, above)
    cross = lax.ppermute(mirror, "zlo", PAIRS)
    left, right = shift(mine, "x", 1), shift(mine, "x", -1)
    left = after(left, below, above, cross)
    below, above = ring(3, cross, below, above)
    far_psi, far_phi = shift(left[:, 0], "x", 1), shift(right[:, 1], "x", -1)
    far_psi = after(far_psi, below, above)

    up, down = shift(below[0], "y", 1), shift(above[1], "y", -1)
    parts[3] += [(up, Ellipsis, 0, 2, full), (down, Ellipsis, 1, 2, full)]
    p_parts = [mine, left, right, far_psi, far_phi]
    p_parts += [shift(part, "core", 1) for part in p_parts]

    out = gram(pos, parts, p_parts)
    return out.reshape(16, SHARE, ROWS).transpose(2, 0, 1)


def solution(mesh):
    torus = Mesh(mesh.devices.reshape(tuple(SIZES[a] for a in AXES)), AXES)
    in_specs = (P(ORB, GRID), P(ORB, GRID), P(ORB, GRID), P(ORB, GRID), P(GRID))
    out_specs = P(GRID, None, ORB)
    return jax.shard_map(
        per_device, mesh=torus, in_specs=in_specs, out_specs=out_specs, check_vma=False
    )
```

```python
import functools

import jax
import jax.numpy as jnp
from jax import lax
from jax.experimental import pallas as pl
from jax.experimental.pallas import tpu as pltpu
from jax.sharding import Mesh, PartitionSpec as P

AXES = ("zhi", "x", "core", "zlo", "y")
SIZES = {"zhi": 2, "x": 4, "core": 2, "zlo": 4, "y": 4}
GRID = ("zhi", "x", "core")
ORB = ("zlo", "y")

NPTS = 768
SHARE = 48
ORBS = 192
HALF = ORBS // 2
REGION = 6144
ROWS = 1024
KSLOT = 4 * ORBS
CHUNK = 1024
TILE = 256
GRAM_VMEM = 24
MIB = 1024 * 1024

PAIRS = [(0, 1), (1, 0), (2, 3), (3, 2)]
MIDDLE = [(1, 2), (2, 1)]
OUTWARD = [(1, 0), (2, 3)]


def shift(value, axis, step):
    n = SIZES[axis]
    return lax.ppermute(value, axis, [(i, (i + step) % n) for i in range(n)])


def after(value, *others):
    return lax.optimization_barrier((value,) + others)[0]


def together(*values):
    return lax.optimization_barrier(values)


def gather_kernel(points_ref, psi_ref, phi_ref, out_ref, acc_ref):
    step = pl.program_id(0)
    columns = lax.broadcasted_iota(jnp.int32, (NPTS, CHUNK), 1) + step * CHUNK
    pick = jnp.where(points_ref[...] == columns, 1.0, 0.0).astype(jnp.bfloat16)
    both = jnp.concatenate([psi_ref[...], phi_ref[...]], axis=0)
    part = lax.dot_general(
        pick, both, (((1,), (1,)), ((), ())), preferred_element_type=jnp.float32
    )

    @pl.when(step == 0)
    def _():
        acc_ref[...] = part

    @pl.when(step > 0)
    def _():
        acc_ref[...] += part

    @pl.when(step == pl.num_programs(0) - 1)
    def _():
        out_ref[...] = acc_ref[...].astype(jnp.bfloat16)


def gather_points(points, psi_region, phi_region):
    steps = REGION // CHUNK
    return pl.pallas_call(
        gather_kernel,
        grid=(steps,),
        in_specs=[
            pl.BlockSpec((NPTS, 1), lambda j: (0, 0)),
            pl.BlockSpec((ORBS, CHUNK), lambda j: (0, j)),
            pl.BlockSpec((ORBS, CHUNK), lambda j: (0, j)),
        ],
        out_specs=pl.BlockSpec((NPTS, 2 * ORBS), lambda j: (0, 0)),
        out_shape=jax.ShapeDtypeStruct((NPTS, 2 * ORBS), jnp.bfloat16),
        scratch_shapes=[pltpu.VMEM((NPTS, 2 * ORBS), jnp.float32)],
        compiler_params=pltpu.CompilerParams(vmem_limit_bytes=56 * MIB),
        cost_estimate=pl.CostEstimate(
            flops=2 * NPTS * REGION * 2 * ORBS, bytes_accessed=2 * ORBS * REGION * 2, transcendentals=0
        ),
        name="gather_points",
    )(points, psi_region, phi_region)


def join_kernel(pos_ref, in_ref, out_ref):
    y = pos_ref[3]
    for e in range(4):
        for m in range(2):
            out_ref[:, m, :, e * ORBS : (e + 1) * ORBS] = in_ref[(y + e) % 4, :, :, m * ORBS : (m + 1) * ORBS]


def join_orbitals(pos, by_y):
    vmem = pl.BlockSpec(memory_space=pltpu.VMEM)
    return pl.pallas_call(
        join_kernel,
        in_specs=[pl.BlockSpec(memory_space=pltpu.SMEM), vmem],
        out_specs=vmem,
        out_shape=jax.ShapeDtypeStruct((4, 2, SHARE, KSLOT), jnp.bfloat16),
        compiler_params=pltpu.CompilerParams(vmem_limit_bytes=8 * MIB),
        name="join_orbitals",
    )(pos, by_y)


def gram_kernel(slots, rows, pieces, n_w, n_p, n_acc, pos_ref, *refs):
    w_refs, p_refs, acc_refs = refs[:n_w], refs[n_w : n_w + n_p], refs[n_w + n_p : n_w + n_p + n_acc]
    out_ref, *scratch = refs[n_w + n_p + n_acc :]
    acc = scratch[0] if scratch else out_ref
    x, core, zlo = pos_ref[0], pos_ref[1], pos_ref[2]
    pair = zlo + 1 - 2 * (zlo % 2)
    which = [zlo, pair, 2 - zlo // 2, 3 - 3 * (zlo // 2)]

    for i, s in enumerate(slots):

        def body(n, _):
            cols = pl.ds(pl.multiple_of(n * TILE, TILE), TILE)
            grams = []
            for m in range(2):
                lhs = []
                for zhi, e, swap in rows:
                    z = zhi * 4 + which[s]
                    if e == 2:
                        lhs.append(p_refs[2 * swap + m][z] if n_p == 4 else p_refs[6 + 2 * swap + m][z])
                    else:
                        lhs.append(p_refs[3 * swap + (0, 2, None, 1)[e]][z, m])
                lhs = jnp.concatenate(lhs, axis=0)
                rhs = jnp.concatenate([w_refs[ref][*index, :, cols] for ref, index in pieces[i][m]], axis=0)
                part = jnp.dot(lhs, rhs, preferred_element_type=jnp.float32)
                if n_acc:
                    part = part + jnp.concatenate([ref[m, :, cols] for ref in acc_refs], axis=0)
                elif i > 0:
                    part = part + acc[m, :, cols]
                grams.append(part)
            if n_acc:
                fitted = (grams[0] * grams[1] * (1.0 / (16 * ORBS))).astype(jnp.bfloat16)
                for j, (zhi, e, swap) in enumerate(rows):
                    out_ref[zhi, (x + e) % 4, (core + swap) % 2, :, cols] = fitted[j * SHARE : (j + 1) * SHARE]
            else:
                for m in range(2):
                    acc[m, :, cols] = grams[m]
            return 0

        lax.fori_loop(0, ROWS // TILE, body, 0)


NEAR_ROWS = [(zhi, e, swap) for zhi in range(2) for e in (0, 1, 3) for swap in range(2)]
FAR_ROWS = [(zhi, 2, swap) for zhi in range(2) for swap in range(2)]


def gram(name, pos, rows, slots, parts, p_parts, accs=()):
    arrays, pieces = [], []
    for s in slots:
        mine = []
        for four in parts[s]:
            row = []
            for array, index in four:
                found = [i for i, a in enumerate(arrays) if a is array]
                if not found:
                    found = [len(arrays)]
                    arrays.append(array)
                row.append((found[0], index))
            mine.append(row)
        pieces.append(mine)
    if accs:
        shape = jax.ShapeDtypeStruct((2, 4, 2, SHARE, ROWS), jnp.bfloat16)
    else:
        shape = jax.ShapeDtypeStruct((2, len(rows) * SHARE, ROWS), jnp.float32)
    vmem = pl.BlockSpec(memory_space=pltpu.VMEM)
    operands = [*arrays, *p_parts, *accs]
    return pl.pallas_call(
        functools.partial(gram_kernel, slots, rows, pieces, len(arrays), len(p_parts), len(accs)),
        in_specs=[pl.BlockSpec(memory_space=pltpu.SMEM)] + [vmem] * len(operands),
        out_specs=vmem,
        out_shape=shape,
        compiler_params=pltpu.CompilerParams(vmem_limit_bytes=GRAM_VMEM * MIB),
        cost_estimate=pl.CostEstimate(
            flops=4 * len(slots) * len(rows) * SHARE * KSLOT * ROWS, bytes_accessed=8 * MIB, transcendentals=0
        ),
        name=name,
    )(pos, *operands)


def per_device(psi_window, phi_window, psi_region, phi_region, points):
    pos = jnp.stack([lax.axis_index(a) for a in ("x", "core", "zlo", "y")]).astype(jnp.int32)

    def sides(slot):
        return shift(slot, "y", 1), shift(slot, "y", -1)

    def across(below, above):
        return shift(below[0], "y", 1), shift(above[1], "y", -1)

    inner = (pos[2] == 1) | (pos[2] == 2)

    def passed_on(value):
        return jnp.where(inner, value, lax.ppermute(value, "zlo", OUTWARD))

    own = jnp.stack([psi_window, phi_window])
    near = lax.ppermute(own, "zlo", PAIRS)
    other = lax.ppermute(own, "zlo", MIDDLE)
    side0 = sides(own)
    order = points.reshape(4, 4, SHARE).transpose(1, 0, 2).reshape(NPTS, 1)
    picked = gather_points(order, psi_region, phi_region).reshape(4, 4, SHARE, 2 * ORBS)
    by_y = lax.all_to_all(picked, "y", 0, 0, tiled=True)
    near, other, *side0, by_y = together(near, other, *side0, by_y)
    side1 = sides(near)
    third = passed_on(other)
    last = lax.ppermute(near, "zlo", MIDDLE)
    cols = join_orbitals(pos, by_y)
    cols = after(cols, third, last, *side1)

    mine = lax.all_to_all(jnp.concatenate([cols, cols]), ("zhi", "zlo"), 0, 0, tiled=True)
    far0 = across(*side0)
    far1 = across(*side1)
    mine, third, *far01 = together(mine, third, *far0, *far1)
    far0, far1 = far01[:2], far01[2:]

    left, right = shift(mine, "x", 1), shift(mine, "x", -1)
    side2 = sides(third)
    last = passed_on(last)
    far2 = across(*side2)
    left, right, last, *far2 = together(left, right, last, *far2)

    side3 = sides(last)
    swapped = [shift(part, "core", 1) for part in (mine, left, right)]
    to_right, to_left = together(left[:, 0], right[:, 1], *swapped)[:2]
    far = [shift(to_right, "x", 1), shift(to_left, "x", -1)]

    parts = []
    for slot, (below, above), ahead in ((own, side0, far0), (near, side1, far1), (third, side2, far2)):
        parts.append([[(slot, (m,)), (above, (m,)), (ahead[m], ()), (below, (m,))] for m in range(2)])
    near_p = [mine, left, right, *swapped]
    near_acc = gram("gram_near", pos, NEAR_ROWS, (0, 1, 2), parts, near_p)
    below, above, near_acc = together(*side3, near_acc)
    far3 = across(below, above)
    far_p = far + [shift(part, "core", 1) for part in far]
    far_acc = gram("gram_far", pos, FAR_ROWS, (0, 1, 2), parts, far_p)
    parts.append([[(last, (m,)), (above, (m,)), (far3[m], ()), (below, (m,))] for m in range(2)])
    out = gram("gram_last", pos, NEAR_ROWS + FAR_ROWS, (3,), parts, near_p + far_p, (near_acc, far_acc))
    return out.reshape(16, SHARE, ROWS).transpose(2, 0, 1)


def solution(mesh):
    torus = Mesh(mesh.devices.reshape(tuple(SIZES[a] for a in AXES)), AXES)
    in_specs = (P(ORB, GRID), P(ORB, GRID), P(ORB, GRID), P(ORB, GRID), P(GRID))
    out_specs = P(GRID, None, ORB)
    return jax.shard_map(
        per_device, mesh=torus, in_specs=in_specs, out_specs=out_specs, check_vma=False
    )
```

```python
import functools

import jax
import jax.numpy as jnp
from jax import lax
from jax.experimental import pallas as pl
from jax.experimental.pallas import tpu as pltpu
from jax.sharding import Mesh, PartitionSpec as P

AXES = ("zhi", "x", "core", "zlo", "y")
SIZES = {"zhi": 2, "x": 4, "core": 2, "zlo": 4, "y": 4}
GRID = ("zhi", "x", "core")
ORB = ("zlo", "y")

NPTS = 768
SHARE = 48
ORBS = 192
HALF = ORBS // 2
REGION = 6144
ROWS = 1024
KSLOT = 4 * ORBS
CHUNK = 1024
TILE = 256
GRAM_VMEM = 24
MIB = 1024 * 1024

PAIRS = [(0, 1), (1, 0), (2, 3), (3, 2)]
MIDDLE = [(1, 2), (2, 1)]
OUTWARD = [(1, 0), (2, 3)]


def shift(value, axis, step):
    n = SIZES[axis]
    return lax.ppermute(value, axis, [(i, (i + step) % n) for i in range(n)])


def after(value, *others):
    return lax.optimization_barrier((value,) + others)[0]


def together(*values):
    return lax.optimization_barrier(values)


def gather_kernel(points_ref, psi_ref, phi_ref, out_ref, acc_ref):
    step = pl.program_id(0)
    columns = lax.broadcasted_iota(jnp.int32, (NPTS, CHUNK), 1) + step * CHUNK
    pick = jnp.where(points_ref[...] == columns, 1.0, 0.0).astype(jnp.bfloat16)
    both = jnp.concatenate([psi_ref[...], phi_ref[...]], axis=0)
    part = lax.dot_general(
        pick, both, (((1,), (1,)), ((), ())), preferred_element_type=jnp.float32
    )

    @pl.when(step == 0)
    def _():
        acc_ref[...] = part

    @pl.when(step > 0)
    def _():
        acc_ref[...] += part

    @pl.when(step == pl.num_programs(0) - 1)
    def _():
        out_ref[...] = acc_ref[...].astype(jnp.bfloat16)


def gather_points(points, psi_region, phi_region):
    steps = REGION // CHUNK
    return pl.pallas_call(
        gather_kernel,
        grid=(steps,),
        in_specs=[
            pl.BlockSpec((NPTS, 1), lambda j: (0, 0)),
            pl.BlockSpec((ORBS, CHUNK), lambda j: (0, j)),
            pl.BlockSpec((ORBS, CHUNK), lambda j: (0, j)),
        ],
        out_specs=pl.BlockSpec((NPTS, 2 * ORBS), lambda j: (0, 0)),
        out_shape=jax.ShapeDtypeStruct((NPTS, 2 * ORBS), jnp.bfloat16),
        scratch_shapes=[pltpu.VMEM((NPTS, 2 * ORBS), jnp.float32)],
        compiler_params=pltpu.CompilerParams(vmem_limit_bytes=56 * MIB),
        cost_estimate=pl.CostEstimate(
            flops=2 * NPTS * REGION * 2 * ORBS, bytes_accessed=2 * ORBS * REGION * 2, transcendentals=0
        ),
        name="gather_points",
    )(points, psi_region, phi_region)


def join_kernel(pos_ref, in_ref, out_ref):
    y = pos_ref[3]
    for e in range(4):
        for m in range(2):
            out_ref[:, m, :, e * ORBS : (e + 1) * ORBS] = in_ref[(y + e) % 4, :, :, m * ORBS : (m + 1) * ORBS]


def join_orbitals(pos, by_y):
    vmem = pl.BlockSpec(memory_space=pltpu.VMEM)
    return pl.pallas_call(
        join_kernel,
        in_specs=[pl.BlockSpec(memory_space=pltpu.SMEM), vmem],
        out_specs=vmem,
        out_shape=jax.ShapeDtypeStruct((4, 2, SHARE, KSLOT), jnp.bfloat16),
        compiler_params=pltpu.CompilerParams(vmem_limit_bytes=8 * MIB),
        name="join_orbitals",
    )(pos, by_y)


def gram_kernel(slots, rows, pieces, n_w, n_p, n_acc, pos_ref, *refs):
    w_refs, p_refs, acc_refs = refs[:n_w], refs[n_w : n_w + n_p], refs[n_w + n_p : n_w + n_p + n_acc]
    out_ref, *scratch = refs[n_w + n_p + n_acc :]
    acc = scratch[0] if scratch else out_ref
    x, core, zlo = pos_ref[0], pos_ref[1], pos_ref[2]
    pair = zlo + 1 - 2 * (zlo % 2)
    which = [zlo, pair, 2 - zlo // 2, 3 - 3 * (zlo // 2)]

    for i, s in enumerate(slots):

        def body(n, _):
            cols = pl.ds(pl.multiple_of(n * TILE, TILE), TILE)
            grams = []
            for m in range(2):
                lhs = []
                for zhi, e, swap in rows:
                    z = zhi * 4 + which[s]
                    if e == 2:
                        lhs.append(p_refs[2 * swap + m][z] if n_p == 4 else p_refs[6 + 2 * swap + m][z])
                    else:
                        lhs.append(p_refs[3 * swap + (0, 2, None, 1)[e]][z, m])
                lhs = jnp.concatenate(lhs, axis=0)
                rhs = jnp.concatenate([w_refs[ref][*index, :, cols] for ref, index in pieces[i][m]], axis=0)
                part = jnp.dot(lhs, rhs, preferred_element_type=jnp.float32)
                if n_acc:
                    part = part + jnp.concatenate([ref[m, :, cols] for ref in acc_refs], axis=0)
                elif i > 0:
                    part = part + acc[m, :, cols]
                grams.append(part)
            if n_acc:
                fitted = (grams[0] * grams[1] * (1.0 / (16 * ORBS))).astype(jnp.bfloat16)
                for j, (zhi, e, swap) in enumerate(rows):
                    out_ref[zhi, (x + e) % 4, (core + swap) % 2, :, cols] = fitted[j * SHARE : (j + 1) * SHARE]
            else:
                for m in range(2):
                    acc[m, :, cols] = grams[m]
            return 0

        lax.fori_loop(0, ROWS // TILE, body, 0)


NEAR_ROWS = [(zhi, e, swap) for zhi in range(2) for e in (0, 1, 3) for swap in range(2)]
FAR_ROWS = [(zhi, 2, swap) for zhi in range(2) for swap in range(2)]


def gram(name, pos, rows, slots, parts, p_parts, accs=()):
    arrays, pieces = [], []
    for s in slots:
        mine = []
        for four in parts[s]:
            row = []
            for array, index in four:
                found = [i for i, a in enumerate(arrays) if a is array]
                if not found:
                    found = [len(arrays)]
                    arrays.append(array)
                row.append((found[0], index))
            mine.append(row)
        pieces.append(mine)
    if accs:
        shape = jax.ShapeDtypeStruct((2, 4, 2, SHARE, ROWS), jnp.bfloat16)
    else:
        shape = jax.ShapeDtypeStruct((2, len(rows) * SHARE, ROWS), jnp.float32)
    vmem = pl.BlockSpec(memory_space=pltpu.VMEM)
    operands = [*arrays, *p_parts, *accs]
    return pl.pallas_call(
        functools.partial(gram_kernel, slots, rows, pieces, len(arrays), len(p_parts), len(accs)),
        in_specs=[pl.BlockSpec(memory_space=pltpu.SMEM)] + [vmem] * len(operands),
        out_specs=vmem,
        out_shape=shape,
        compiler_params=pltpu.CompilerParams(vmem_limit_bytes=GRAM_VMEM * MIB),
        cost_estimate=pl.CostEstimate(
            flops=4 * len(slots) * len(rows) * SHARE * KSLOT * ROWS, bytes_accessed=8 * MIB, transcendentals=0
        ),
        name=name,
    )(pos, *operands)


def per_device(psi_window, phi_window, psi_region, phi_region, points):
    pos = jnp.stack([lax.axis_index(a) for a in ("x", "core", "zlo", "y")]).astype(jnp.int32)

    def sides(slot):
        return shift(slot, "y", 1), shift(slot, "y", -1)

    def across(below, above):
        return shift(below[0], "y", 1), shift(above[1], "y", -1)

    inner = (pos[2] == 1) | (pos[2] == 2)

    def passed_on(value):
        return jnp.where(inner, value, lax.ppermute(value, "zlo", OUTWARD))

    own = jnp.stack([psi_window, phi_window])
    near = lax.ppermute(own, "zlo", PAIRS)
    other = lax.ppermute(own, "zlo", MIDDLE)
    side0 = sides(own)
    order = points.reshape(4, 4, SHARE).transpose(1, 0, 2).reshape(NPTS, 1)
    picked = gather_points(order, psi_region, phi_region).reshape(4, 4, SHARE, 2 * ORBS)
    near, other, *side0, picked = together(near, other, *side0, picked)
    by_y = lax.all_to_all(picked, "y", 0, 0, tiled=True)
    side1 = sides(near)
    third = passed_on(other)
    last = lax.ppermute(near, "zlo", MIDDLE)
    cols = join_orbitals(pos, by_y)
    cols = after(cols, third, last, *side1)

    mine = lax.all_to_all(jnp.concatenate([cols, cols]), ("zhi", "zlo"), 0, 0, tiled=True)
    far0 = across(*side0)
    far1 = across(*side1)
    mine, third, *far01 = together(mine, third, *far0, *far1)
    far0, far1 = far01[:2], far01[2:]

    left, right = shift(mine, "x", 1), shift(mine, "x", -1)
    side2 = sides(third)
    last = passed_on(last)
    far2 = across(*side2)
    left, right, last, *far2 = together(left, right, last, *far2)

    side3 = sides(last)
    swapped = [shift(part, "core", 1) for part in (mine, left, right)]
    to_right, to_left = together(left[:, 0], right[:, 1], *swapped)[:2]
    far = [shift(to_right, "x", 1), shift(to_left, "x", -1)]

    parts = []
    for slot, (below, above), ahead in ((own, side0, far0), (near, side1, far1), (third, side2, far2)):
        parts.append([[(slot, (m,)), (above, (m,)), (ahead[m], ()), (below, (m,))] for m in range(2)])
    near_p = [mine, left, right, *swapped]
    near_acc = gram("gram_near", pos, NEAR_ROWS, (0, 1, 2), parts, near_p)
    below, above, near_acc = together(*side3, near_acc)
    far3 = across(below, above)
    far_p = far + [shift(part, "core", 1) for part in far]
    far_acc = gram("gram_far", pos, FAR_ROWS, (0, 1, 2), parts, far_p)
    parts.append([[(last, (m,)), (above, (m,)), (far3[m], ()), (below, (m,))] for m in range(2)])
    out = gram("gram_last", pos, NEAR_ROWS + FAR_ROWS, (3,), parts, near_p + far_p, (near_acc, far_acc))
    return out.reshape(16, SHARE, ROWS).transpose(2, 0, 1)


def solution(mesh):
    torus = Mesh(mesh.devices.reshape(tuple(SIZES[a] for a in AXES)), AXES)
    in_specs = (P(ORB, GRID), P(ORB, GRID), P(ORB, GRID), P(ORB, GRID), P(GRID))
    out_specs = P(GRID, None, ORB)
    return jax.shard_map(
        per_device, mesh=torus, in_specs=in_specs, out_specs=out_specs, check_vma=False
    )
```

```python
import functools

import jax
import jax.numpy as jnp
from jax import lax
from jax.experimental import pallas as pl
from jax.experimental.pallas import tpu as pltpu
from jax.sharding import Mesh, PartitionSpec as P

AXES = ("zhi", "x", "core", "zlo", "y")
SIZES = {"zhi": 2, "x": 4, "core": 2, "zlo": 4, "y": 4}
GRID = ("zhi", "x", "core")
ORB = ("zlo", "y")

NPTS = 768
SHARE = 48
ORBS = 192
HALF = ORBS // 2
REGION = 6144
ROWS = 1024
KSLOT = 4 * ORBS
CHUNK = 1024
TILE = 512
GRAM_VMEM = 32
MIB = 1024 * 1024

PAIRS = [(0, 1), (1, 0), (2, 3), (3, 2)]
MIDDLE = [(1, 2), (2, 1)]
OUTWARD = [(1, 0), (2, 3)]


def shift(value, axis, step):
    n = SIZES[axis]
    return lax.ppermute(value, axis, [(i, (i + step) % n) for i in range(n)])


def after(value, *others):
    return lax.optimization_barrier((value,) + others)[0]


def together(*values):
    return lax.optimization_barrier(values)


def gather_kernel(points_ref, psi_ref, phi_ref, out_ref, acc_ref):
    step = pl.program_id(0)
    columns = lax.broadcasted_iota(jnp.int32, (NPTS, CHUNK), 1) + step * CHUNK
    pick = jnp.where(points_ref[...] == columns, 1.0, 0.0).astype(jnp.bfloat16)
    both = jnp.concatenate([psi_ref[...], phi_ref[...]], axis=0)
    part = lax.dot_general(
        pick, both, (((1,), (1,)), ((), ())), preferred_element_type=jnp.float32
    )

    @pl.when(step == 0)
    def _():
        acc_ref[...] = part

    @pl.when(step > 0)
    def _():
        acc_ref[...] += part

    @pl.when(step == pl.num_programs(0) - 1)
    def _():
        out_ref[...] = acc_ref[...].astype(jnp.bfloat16)


def gather_points(points, psi_region, phi_region):
    steps = REGION // CHUNK
    return pl.pallas_call(
        gather_kernel,
        grid=(steps,),
        in_specs=[
            pl.BlockSpec((NPTS, 1), lambda j: (0, 0)),
            pl.BlockSpec((ORBS, CHUNK), lambda j: (0, j)),
            pl.BlockSpec((ORBS, CHUNK), lambda j: (0, j)),
        ],
        out_specs=pl.BlockSpec((NPTS, 2 * ORBS), lambda j: (0, 0)),
        out_shape=jax.ShapeDtypeStruct((NPTS, 2 * ORBS), jnp.bfloat16),
        scratch_shapes=[pltpu.VMEM((NPTS, 2 * ORBS), jnp.float32)],
        compiler_params=pltpu.CompilerParams(vmem_limit_bytes=56 * MIB),
        cost_estimate=pl.CostEstimate(
            flops=2 * NPTS * REGION * 2 * ORBS, bytes_accessed=2 * ORBS * REGION * 2, transcendentals=0
        ),
        name="gather_points",
    )(points, psi_region, phi_region)


def join_kernel(pos_ref, in_ref, out_ref):
    y = pos_ref[3]
    for e in range(4):
        for m in range(2):
            out_ref[:, m, :, e * ORBS : (e + 1) * ORBS] = in_ref[(y + e) % 4, :, :, m * ORBS : (m + 1) * ORBS]


def join_orbitals(pos, by_y):
    vmem = pl.BlockSpec(memory_space=pltpu.VMEM)
    return pl.pallas_call(
        join_kernel,
        in_specs=[pl.BlockSpec(memory_space=pltpu.SMEM), vmem],
        out_specs=vmem,
        out_shape=jax.ShapeDtypeStruct((4, 2, SHARE, KSLOT), jnp.bfloat16),
        compiler_params=pltpu.CompilerParams(vmem_limit_bytes=8 * MIB),
        name="join_orbitals",
    )(pos, by_y)


def gram_kernel(slots, rows, pieces, n_w, n_p, n_acc, pos_ref, *refs):
    w_refs, p_refs, acc_refs = refs[:n_w], refs[n_w : n_w + n_p], refs[n_w + n_p : n_w + n_p + n_acc]
    out_ref, *scratch = refs[n_w + n_p + n_acc :]
    acc = scratch[0] if scratch else out_ref
    x, core, zlo = pos_ref[0], pos_ref[1], pos_ref[2]
    pair = zlo + 1 - 2 * (zlo % 2)
    which = [zlo, pair, 2 - zlo // 2, 3 - 3 * (zlo // 2)]

    for i, s in enumerate(slots):

        def body(n, _):
            cols = pl.ds(pl.multiple_of(n * TILE, TILE), TILE)
            grams = []
            for m in range(2):
                lhs = []
                for zhi, e, swap in rows:
                    z = zhi * 4 + which[s]
                    if e == 2:
                        lhs.append(p_refs[2 * swap + m][z] if n_p == 4 else p_refs[6 + 2 * swap + m][z])
                    else:
                        lhs.append(p_refs[3 * swap + (0, 2, None, 1)[e]][z, m])
                lhs = jnp.concatenate(lhs, axis=0)
                rhs = jnp.concatenate([w_refs[ref][*index, :, cols] for ref, index in pieces[i][m]], axis=0)
                part = jnp.dot(lhs, rhs, preferred_element_type=jnp.float32)
                if n_acc:
                    part = part + jnp.concatenate([ref[m, :, cols] for ref in acc_refs], axis=0)
                elif i > 0:
                    part = part + acc[m, :, cols]
                grams.append(part)
            if n_acc:
                fitted = (grams[0] * grams[1] * (1.0 / (16 * ORBS))).astype(jnp.bfloat16)
                for j, (zhi, e, swap) in enumerate(rows):
                    out_ref[zhi, (x + e) % 4, (core + swap) % 2, :, cols] = fitted[j * SHARE : (j + 1) * SHARE]
            else:
                for m in range(2):
                    acc[m, :, cols] = grams[m]
            return 0

        lax.fori_loop(0, ROWS // TILE, body, 0)


NEAR_ROWS = [(zhi, e, swap) for zhi in range(2) for e in (0, 1, 3) for swap in range(2)]
FAR_ROWS = [(zhi, 2, swap) for zhi in range(2) for swap in range(2)]


def gram(name, pos, rows, slots, parts, p_parts, accs=()):
    arrays, pieces = [], []
    for s in slots:
        mine = []
        for four in parts[s]:
            row = []
            for array, index in four:
                found = [i for i, a in enumerate(arrays) if a is array]
                if not found:
                    found = [len(arrays)]
                    arrays.append(array)
                row.append((found[0], index))
            mine.append(row)
        pieces.append(mine)
    if accs:
        shape = jax.ShapeDtypeStruct((2, 4, 2, SHARE, ROWS), jnp.bfloat16)
    else:
        shape = jax.ShapeDtypeStruct((2, len(rows) * SHARE, ROWS), jnp.float32)
    vmem = pl.BlockSpec(memory_space=pltpu.VMEM)
    operands = [*arrays, *p_parts, *accs]
    return pl.pallas_call(
        functools.partial(gram_kernel, slots, rows, pieces, len(arrays), len(p_parts), len(accs)),
        in_specs=[pl.BlockSpec(memory_space=pltpu.SMEM)] + [vmem] * len(operands),
        out_specs=vmem,
        out_shape=shape,
        compiler_params=pltpu.CompilerParams(vmem_limit_bytes=GRAM_VMEM * MIB),
        cost_estimate=pl.CostEstimate(
            flops=4 * len(slots) * len(rows) * SHARE * KSLOT * ROWS, bytes_accessed=8 * MIB, transcendentals=0
        ),
        name=name,
    )(pos, *operands)


def per_device(psi_window, phi_window, psi_region, phi_region, points):
    pos = jnp.stack([lax.axis_index(a) for a in ("x", "core", "zlo", "y")]).astype(jnp.int32)

    def sides(slot):
        return shift(slot, "y", 1), shift(slot, "y", -1)

    def across(below, above):
        return shift(below[0], "y", 1), shift(above[1], "y", -1)

    inner = (pos[2] == 1) | (pos[2] == 2)

    def passed_on(value):
        return jnp.where(inner, value, lax.ppermute(value, "zlo", OUTWARD))

    own = jnp.stack([psi_window, phi_window])
    near = lax.ppermute(own, "zlo", PAIRS)
    other = lax.ppermute(own, "zlo", MIDDLE)
    side0 = sides(own)
    order = points.reshape(4, 4, SHARE).transpose(1, 0, 2).reshape(NPTS, 1)
    picked = gather_points(order, psi_region, phi_region).reshape(4, 4, SHARE, 2 * ORBS)
    near, other, *side0, picked = together(near, other, *side0, picked)
    by_y = lax.all_to_all(picked, "y", 0, 0, tiled=True)
    side1 = sides(near)
    third = passed_on(other)
    last = lax.ppermute(near, "zlo", MIDDLE)
    cols = join_orbitals(pos, by_y)
    cols = after(cols, third, last, *side1)

    mine = lax.all_to_all(jnp.concatenate([cols, cols]), ("zhi", "zlo"), 0, 0, tiled=True)
    far0 = across(*side0)
    far1 = across(*side1)
    mine, third, *far01 = together(mine, third, *far0, *far1)
    far0, far1 = far01[:2], far01[2:]

    left, right = shift(mine, "x", 1), shift(mine, "x", -1)
    side2 = sides(third)
    last = passed_on(last)
    far2 = across(*side2)
    left, right, last, *far2 = together(left, right, last, *far2)

    side3 = sides(last)
    swapped = [shift(part, "core", 1) for part in (mine, left, right)]
    to_right, to_left = together(left[:, 0], right[:, 1], *swapped)[:2]
    far = [shift(to_right, "x", 1), shift(to_left, "x", -1)]

    parts = []
    for slot, (below, above), ahead in ((own, side0, far0), (near, side1, far1), (third, side2, far2)):
        parts.append([[(slot, (m,)), (above, (m,)), (ahead[m], ()), (below, (m,))] for m in range(2)])
    near_p = [mine, left, right, *swapped]
    near_acc = gram("gram_near", pos, NEAR_ROWS, (0, 1, 2), parts, near_p)
    below, above, near_acc = together(*side3, near_acc)
    far3 = across(below, above)
    far_p = far + [shift(part, "core", 1) for part in far]
    far_acc = gram("gram_far", pos, FAR_ROWS, (0, 1, 2), parts, far_p)
    parts.append([[(last, (m,)), (above, (m,)), (far3[m], ()), (below, (m,))] for m in range(2)])
    out = gram("gram_last", pos, NEAR_ROWS + FAR_ROWS, (3,), parts, near_p + far_p, (near_acc, far_acc))
    return out.reshape(16, SHARE, ROWS).transpose(2, 0, 1)


def solution(mesh):
    torus = Mesh(mesh.devices.reshape(tuple(SIZES[a] for a in AXES)), AXES)
    in_specs = (P(ORB, GRID), P(ORB, GRID), P(ORB, GRID), P(ORB, GRID), P(GRID))
    out_specs = P(GRID, None, ORB)
    return jax.shard_map(
        per_device, mesh=torus, in_specs=in_specs, out_specs=out_specs, check_vma=False
    )
```
